32 devices in a mesh: groups: 2 (over x), sector: 16 (over z, y, core).
Axes of the slice: x: 2, y: 2, z: 4, core: 2. Of those that a mesh axis runs over, the one named last changes fastest.
Arguments:
- wavefunction: bfloat16 [256, 4, 128, 128], P(('groups', 'sector')), parts along dimension 0, may hold values from -46 to 46
- left_env: bfloat16 [16, 256, 128, 128], P(None, ('groups', 'sector')), parts along dimension 1, may hold values from -2 to 2
- right_env: bfloat16 [16, 256, 128, 128], P(None, ('groups', 'sector')), parts along dimension 1, may hold values from -2 to 2
- energy_diag: float32 [256, 4, 128, 128], P(('groups', 'sector')), parts along dimension 0, may hold values from -1 to 1.5
- sector_dims: int32 [2, 128], replicated, may hold values from 32 to 128
- pair_table: int32 [128, 4], replicated, may hold values from 0 to 127, as said below
Outputs:
- sigma_blocks: bfloat16 [256, 4, 128, 128], P(('groups', 'sector')), parts along dimension 0
- correction: float32 [256, 4, 128, 128], P(('groups', 'sector')), parts along dimension 0
The draws below stay inside these ranges and needn't reach their ends.
There are 2 independent parts, one for each index of `groups`. The reference program is written for one: setup_inputs(seed, part) draws one part's arguments, and reference() takes and returns one part's arrays. A program takes and returns all parts, laid end to end along the dimension named above; an argument that names none is the same for every part. Nothing has to cross between parts.
Inputs may be any that keep to these rules, and one draw needn't show every extreme that they name: `pair_table`: right sector b is held by index b // 8 of sector. The 4 right sectors of one left sector are distinct. Among the blocks of the 8 left sectors of one index of sector, at most 4 have right sectors held by any one index; in every draw some index of sector holds the right sectors of exactly 4 blocks from every index.
All inputs are finite; a program needn't handle non-finite values.
Results may differ from the reference program's by a relative error of at most 0.0068.
Values may be sent and summed in bfloat16 or wider, within the bound.
A program may use at most 256 MiB of HBM per device.

```python
import math
import jax
import jax.numpy as jnp
from jax import lax

B = 128
K = 4
W = 16
SEC_DEV = 8
NSEC = 128
CAP = 4


def draw_wavefunction(key, part):
    key = jax.random.fold_in(key, 11)
    key_base, key_rows, key_cols = jax.random.split(key, 3)
    shape = (NSEC, K, B, B)
    base = jnp.clip(jax.random.normal(key_base, shape, jnp.float32), -4.0, 4.0)
    climb = 3.0
    half_decade = 0.5 * math.log(10.0)
    row_scale = jnp.exp(jax.random.uniform(key_rows, (NSEC, K, B, 1), jnp.float32, 0.0, 1.0) * half_decade)
    col_scale = jnp.exp(jax.random.uniform(key_cols, (NSEC, K, 1, B), jnp.float32, 0.0, 1.0) * half_decade)
    placing = jnp.arange(NSEC, dtype=jnp.float32) / (NSEC - 1)
    rising = jnp.exp(math.log(climb) * placing)[:, None, None, None]
    return (0.3 * base * row_scale * col_scale * rising).astype(jnp.bfloat16)


def environment(noise, key_level):
    level = jax.random.uniform(key_level, (W, NSEC, 1, 1), jnp.float32, 0.3, 1.0)
    identity = (jnp.arange(B)[:, None] == jnp.arange(B)[None, :]).astype(jnp.float32)
    return ((level * identity + noise / math.sqrt(B)) / math.sqrt(W)).astype(jnp.bfloat16)


def draw_left_env(key, part):
    key = jax.random.fold_in(key, 21)
    key_noise, key_level = jax.random.split(key)
    shape = (W, NSEC, B, B)
    noise = jnp.clip(jax.random.normal(key_noise, shape, jnp.float32), -4.0, 4.0)
    return environment(noise, key_level)


def draw_right_env(key, part):
    key = jax.random.fold_in(key, 22)
    key_noise, key_level = jax.random.split(key)
    shape = (W, NSEC, B, B)
    noise = jnp.clip(jax.random.normal(key_noise, shape, jnp.float32), -4.0, 4.0)
    return environment(noise, key_level)


def draw_sector_dims(key, part):
    key = jax.random.fold_in(key, 31)
    key_dims, key_spot = jax.random.split(key)
    dims_drawn = jax.random.randint(key_dims, (2, NSEC), B // 4, B + 1)
    spot = jax.random.randint(key_spot, (2, 1), 0, NSEC)
    widest = jnp.arange(NSEC)[None, :] == spot
    return jnp.where(widest, B, dims_drawn).astype(jnp.int32)


def draw_pair_table(key, part):
    key = jax.random.fold_in(key, 41)
    owner_total = NSEC // SEC_DEV
    block_total = SEC_DEV * K
    slot_total = owner_total * CAP
    key_busy, key_rows = jax.random.split(key)
    busiest = jax.random.randint(key_busy, (), 0, owner_total)
    slot_owner = jnp.arange(slot_total, dtype=jnp.int32) // CAP
    slot_order = jnp.arange(slot_total, dtype=jnp.int32) % CAP

    def one_source(source_key):
        key_rank, key_shuffle, key_offset = jax.random.split(source_key, 3)
        ranking = jax.random.permutation(key_rank, slot_total).astype(jnp.int32)
        priority = jnp.where(slot_owner == busiest, slot_order, CAP + ranking)
        chosen = jnp.argsort(priority, stable=True)[:block_total]
        shuffle = jax.random.permutation(key_shuffle, block_total)
        chosen = chosen[shuffle]
        offsets = jax.random.randint(key_offset, (owner_total,), 0, SEC_DEV)
        owner_index = slot_owner[chosen]
        within = (slot_order[chosen] + offsets[owner_index]) % SEC_DEV
        return (owner_index * SEC_DEV + within).reshape(SEC_DEV, K)
    table = jax.vmap(one_source)(jax.random.split(key_rows, owner_total))
    return table.reshape(NSEC, K).astype(jnp.int32)


def level_of(rng, extent, shards, low, top_value):
    gain, own = 1.0, jax.random.fold_in(rng, 6)
    for position, shards_of in shards:
        heights = jnp.exp(jax.random.uniform(jax.random.fold_in(own, position), (shards_of,), jnp.float32, low / len(shards), top_value / len(shards)))
        gain = gain * jnp.repeat(heights, extent[position] // shards_of).reshape([-1 if axis == position else 1 for axis in range(len(extent))])
    return gain


def setup_inputs(seed: int = 0, part: int = 0) -> dict:
    key_list = jax.random.split(jax.random.key(seed), 7)
    part_keys = jax.random.split(jax.random.fold_in(key_list[6], part), 7)
    wavefunction = draw_wavefunction(jax.random.fold_in(jax.random.fold_in(key_list[6], part), 71), part)
    left_env = draw_left_env(jax.random.fold_in(jax.random.fold_in(key_list[6], part), 71), part)
    right_env = draw_right_env(jax.random.fold_in(jax.random.fold_in(key_list[6], part), 71), part)
    energy_diag = jnp.clip(-1.0 + 2.5 * jax.random.uniform(part_keys[3], (NSEC, K, B, B), jnp.float32) ** level_of(part_keys[3], (NSEC, K, B, B), ((0, 16),), -0.2, 0.2), -1.0, 1.5)
    sector_dims = draw_sector_dims(jax.random.fold_in(key_list[6], 71), part)
    pair_table = draw_pair_table(jax.random.fold_in(key_list[6], 71), part)
    return dict(wavefunction=wavefunction, left_env=left_env, right_env=right_env, energy_diag=energy_diag, sector_dims=sector_dims, pair_table=pair_table)


def reference(wavefunction, left_env, right_env, energy_diag, sector_dims, pair_table):
    positions = jnp.arange(B, dtype=jnp.int32)

    def one_sector(sector_index):
        block_psi = wavefunction[sector_index]
        left_dim = sector_dims[0, sector_index]
        partner = pair_table[sector_index]
        right_dim = sector_dims[1][partner]
        live_mask = ((positions[None, :, None] < left_dim) & (positions[None, None, :] < right_dim[:, None, None])).astype(jnp.bfloat16)
        masked = block_psi * live_mask
        left_block = left_env[:, sector_index].astype(jnp.float32)
        partial_blocks = jnp.einsum("wij,kjl->wkil", left_block, masked.astype(jnp.float32)).astype(jnp.bfloat16)
        right_block = right_env[:, partner].astype(jnp.float32)
        summed = jnp.einsum("wkil,wkml->kim", partial_blocks.astype(jnp.float32), right_block)
        sigma_part = summed.astype(jnp.bfloat16) * live_mask
        return masked, sigma_part

    masked, sigma_blocks = lax.map(one_sector, jnp.arange(NSEC, dtype=jnp.int32))
    masked_wide = masked.astype(jnp.float32)
    sigma_wide = sigma_blocks.astype(jnp.float32)
    correlation = jnp.sum(masked_wide * sigma_wide)
    norm_sum = jnp.sum(masked_wide * masked_wide)
    quotient = correlation / norm_sum
    residual = sigma_wide - quotient * masked_wide
    distance = quotient - energy_diag
    correction = residual * distance / (distance * distance + 0.25)
    return sigma_blocks, correction
```

```python
import functools
import jax
import jax.numpy as jnp
from jax import lax
from jax.experimental import pallas as pl
from jax.experimental.pallas import tpu as pltpu
from jax.sharding import PartitionSpec as P

TEAM = 4
PARTS = 2


def exchange_kernel(lines, terms, left_ref, right_ref, wave_ref, left_all, right_all, wave_all,
                    team_send, team_recv, side_send, side_recv, line_send, line_recv, local_sem):
    me = lax.axis_index("sector")
    line = me // TEAM
    member = me % TEAM
    half = terms // PARTS
    pieces = TEAM * PARTS

    def peer(x):
        return ((member // 2 + x // 2) % 2) * 2 + (member % 2 + x % 2) % 2

    barrier = pltpu.get_barrier_semaphore()

    def greet(who):
        pl.semaphore_signal(barrier, inc=1, device_id={"sector": who},
                            device_id_type=pl.DeviceIdType.MESH)

    for x in range(1, TEAM):
        greet(line * TEAM + peer(x))

    @pl.when(line > 0)
    def _():
        greet(me - TEAM)

    @pl.when(line < lines - 1)
    def _():
        greet(me + TEAM)

    ends = (line == 0).astype(jnp.int32) + (line == lines - 1).astype(jnp.int32)
    pl.semaphore_wait(barrier, TEAM + 1 - ends)

    def remote(src, dst, send, recv, who):
        return pltpu.make_async_remote_copy(
            src_ref=src, dst_ref=dst, send_sem=send, recv_sem=recv,
            device_id={"sector": who}, device_id_type=pl.DeviceIdType.MESH)

    def team_copy(x, part):
        q = x * PARTS + part
        other = peer(x)
        return remote(right_ref.at[pl.ds(other * terms + part * half, half)],
                      right_all.at[me, pl.ds(part * half, half)],
                      team_send.at[q], team_recv.at[q], line * TEAM + other)

    def left_copy(x):
        other = peer(x)
        return remote(left_ref.at[pl.ds(other * terms, terms)], left_all.at[member],
                      side_send.at[0, x], side_recv.at[0, x], line * TEAM + other)

    def wave_copy(x):
        other = peer(x)
        return remote(wave_ref, wave_all.at[member],
                      side_send.at[1, x], side_recv.at[1, x], line * TEAM + other)

    def line_copy(up, hop, q):
        x, part = q // PARTS, q % PARTS
        step = 1 if up else -1
        origin = (line - step * (hop - 1)) * TEAM + peer(x)
        there = right_all.at[origin, pl.ds(part * half, half)]
        if hop == 1 and x == 0:
            src = right_ref.at[pl.ds(member * terms + part * half, half)]
        else:
            src = there
        side = 0 if up else 1
        return remote(src, there, line_send.at[side, hop - 1, q],
                      line_recv.at[side, hop - 1, q], me + step * TEAM)

    def can_send(up, hop):
        if up:
            return (line >= hop - 1) & (line < lines - 1)
        return (line + hop - 1 < lines) & (line > 0)

    keep = [
        pltpu.make_async_copy(right_ref.at[pl.ds(member * terms, terms)], right_all.at[me], local_sem.at[0]),
        pltpu.make_async_copy(left_ref.at[pl.ds(member * terms, terms)], left_all.at[member], local_sem.at[1]),
        pltpu.make_async_copy(wave_ref, wave_all.at[member], local_sem.at[2]),
    ]
    for q in range(PARTS, pieces):
        team_copy(q // PARTS, q % PARTS).start()
    for slot in range(pieces + lines - 2):
        for hop in range(1, lines):
            q = slot - (hop - 1)
            if not 0 <= q < pieces:
                continue
            if hop == 1 and q >= PARTS:
                team_copy(q // PARTS, q % PARTS).wait_recv()
            for up in (True, False):
                @pl.when(can_send(up, hop))
                def _():
                    if hop > 1:
                        line_copy(up, hop - 1, q).wait_recv()
                    line_copy(up, hop, q).start()
        if slot == PARTS - 1:
            for copy in keep:
                copy.start()
            for x in range(1, TEAM):
                left_copy(x).start()
                wave_copy(x).start()
    for q in range(pieces):
        for hop in range(1, lines):
            for up in (True, False):
                end = lines - 1 if up else 0
                from_there = (line >= hop) if up else (line + hop < lines)

                @pl.when((line == end) & from_there)
                def _():
                    line_copy(up, hop, q).wait_recv()

                @pl.when(can_send(up, hop))
                def _():
                    line_copy(up, hop, q).wait_send()
    for q in range(PARTS, pieces):
        team_copy(q // PARTS, q % PARTS).wait_send()
    for x in range(1, TEAM):
        left_copy(x).wait()
        wave_copy(x).wait()
    for copy in keep:
        copy.wait()


def exchange(wave, left_env, right_env, peer_count):
    total, sectors, size, _ = left_env.shape
    terms = total // TEAM
    lines = peer_count // TEAM
    pieces = TEAM * PARTS
    dma = pltpu.SemaphoreType.DMA
    hbm = pl.BlockSpec(memory_space=pl.ANY)
    return pl.pallas_call(
        functools.partial(exchange_kernel, lines, terms),
        out_shape=(
            jax.ShapeDtypeStruct((TEAM, terms, sectors, size, size), left_env.dtype),
            jax.ShapeDtypeStruct((peer_count, terms, sectors, size, size), right_env.dtype),
            jax.ShapeDtypeStruct((TEAM,) + wave.shape, wave.dtype),
        ),
        in_specs=[hbm] * 3,
        out_specs=(hbm, hbm, hbm),
        scratch_shapes=[
            dma((pieces,)), dma((pieces,)),
            dma((2, TEAM)), dma((2, TEAM)),
            dma((2, lines - 1, pieces)), dma((2, lines - 1, pieces)),
            dma((3,)),
        ],
        compiler_params=pltpu.CompilerParams(collective_id=0, has_side_effects=True),
        name="exchange",
    )(left_env, right_env, wave)


def products_kernel(partners, terms, pairs_ref, rows_ref, cols_ref, left_ref, wave_ref, *rest):
    right_refs, out_ref = rest[:partners], rest[partners]
    size = wave_ref.shape[-1]
    step = pl.program_id(0)
    row_ids = lax.broadcasted_iota(jnp.int32, (size, size), 0)
    col_ids = lax.broadcasted_iota(jnp.int32, (size, size), 1)
    masked = []
    for k in range(partners):
        live = (row_ids < rows_ref[step]) & (col_ids < cols_ref[step * partners + k])
        masked.append(jnp.where(live, wave_ref[0, 0, k], jnp.zeros((), wave_ref.dtype)))
    masked = jnp.concatenate(masked, axis=1)
    halves = [jnp.dot(left_ref[0, w, 0], masked, preferred_element_type=jnp.float32).astype(jnp.bfloat16)
              for w in range(terms)]
    for k in range(partners):
        first = jnp.concatenate([p[:, k * size:(k + 1) * size] for p in halves], axis=1)
        second = jnp.concatenate([right_refs[k][0, w, 0] for w in range(terms)], axis=1)
        out_ref[0, 0, k] = lax.dot_general(
            first, second, (((1,), (1,)), ((), ())), preferred_element_type=jnp.float32
        ).astype(out_ref.dtype)


def products(pairs, rows, cols, left_all, right_all, wave_all):
    team, sectors, partners, size, _ = wave_all.shape
    terms = left_all.shape[1]

    def pick(k):
        def index(i, pairs_ref, rows_ref, cols_ref):
            b = pairs_ref[i * partners + k]
            return (b // sectors, 0, b % sectors, 0, 0)
        return pl.BlockSpec((1, terms, 1, size, size), index)

    def own(i, *_):
        return (i // sectors, i % sectors, 0, 0, 0)

    blocks = team * sectors * partners
    return pl.pallas_call(
        functools.partial(products_kernel, partners, terms),
        grid_spec=pltpu.PrefetchScalarGridSpec(
            num_scalar_prefetch=3,
            grid=(team * sectors,),
            in_specs=[
                pl.BlockSpec((1, terms, 1, size, size), lambda i, *_: (i // sectors, 0, i % sectors, 0, 0)),
                pl.BlockSpec((1, 1, partners, size, size), own),
            ] + [pick(k) for k in range(partners)],
            out_specs=pl.BlockSpec((1, 1, partners, size, size), own),
        ),
        out_shape=jax.ShapeDtypeStruct(wave_all.shape, jnp.bfloat16),
        compiler_params=pltpu.CompilerParams(vmem_limit_bytes=32 * 1024 * 1024),
        cost_estimate=pl.CostEstimate(flops=4 * blocks * terms * size ** 3,
                                      bytes_accessed=28 * 2 ** 20, transcendentals=0),
        name="products",
    )(pairs, rows, cols, left_all, wave_all, *([right_all] * partners))


def body(wavefunction, left_env, right_env, energy_diag, sector_dims, pair_table):
    local_sectors = wavefunction.shape[0]
    tile_size = wavefunction.shape[2]
    peer_count = lax.axis_size("sector")
    my_index = lax.axis_index("sector")
    line = my_index // TEAM
    team_sectors = TEAM * local_sectors
    team_first = line * team_sectors
    team_pairs = lax.dynamic_slice_in_dim(pair_table, team_first, team_sectors, 0)
    team_rows = lax.dynamic_slice_in_dim(sector_dims[0], team_first, team_sectors, 0)
    team_cols = jnp.take(sector_dims[1], team_pairs)
    left_all, right_all, wave_all = exchange(wavefunction, left_env, right_env, peer_count)
    sums = products(team_pairs.reshape(-1), team_rows, team_cols.reshape(-1), left_all, right_all, wave_all)
    teams = [[g * TEAM + i for i in range(TEAM)] for g in range(peer_count // TEAM)]
    arrived = lax.all_to_all(sums, "sector", split_axis=0, concat_axis=0, axis_index_groups=teams, tiled=True)
    summed = jnp.sum(arrived.astype(jnp.float32), axis=0)
    member_first = (my_index % TEAM) * local_sectors
    left_dims = lax.dynamic_slice_in_dim(team_rows, member_first, local_sectors, 0)
    right_dims = lax.dynamic_slice_in_dim(team_cols, member_first, local_sectors, 0)
    positions = jnp.arange(tile_size, dtype=jnp.int32)
    live = (positions[None, None, :, None] < left_dims[:, None, None, None]) & (
        positions[None, None, None, :] < right_dims[:, :, None, None])
    masked_wide = jnp.where(live, wavefunction.astype(jnp.float32), 0.0)
    sigma_blocks = jnp.where(live, summed, 0.0).astype(jnp.bfloat16)
    sigma_wide = sigma_blocks.astype(jnp.float32)
    correlation, norm_sum = lax.psum(
        (jnp.sum(masked_wide * sigma_wide), jnp.sum(masked_wide * masked_wide)), "sector")
    quotient = correlation / norm_sum
    residual = sigma_wide - quotient * masked_wide
    distance = quotient - energy_diag
    correction = residual * distance / (distance * distance + 0.25)
    return (sigma_blocks, correction)


def solution(mesh):
    blocks = P(("groups", "sector"), None, None, None)
    environments = P(None, ("groups", "sector"), None, None)
    return jax.shard_map(
        body,
        mesh=mesh,
        in_specs=(blocks, environments, environments, blocks, P(), P()),
        out_specs=(blocks, blocks),
        check_vma=False,
    )
```

```python
import functools
import jax
import jax.numpy as jnp
from jax import lax
from jax.experimental import pallas as pl
from jax.experimental.pallas import tpu as pltpu
from jax.sharding import PartitionSpec as P

TEAM = 4
PARTS = 2


def exchange_kernel(lines, terms, left_ref, right_ref, wave_ref, left_all, right_all, wave_all,
                    team_send, team_recv, side_send, side_recv, line_send, line_recv, local_sem):
    me = lax.axis_index("sector")
    line = me // TEAM
    member = me % TEAM
    half = terms // PARTS
    pieces = TEAM * PARTS

    def peer(x):
        return ((member // 2 + x // 2) % 2) * 2 + (member % 2 + x % 2) % 2

    barrier = pltpu.get_barrier_semaphore()

    def greet(who):
        pl.semaphore_signal(barrier, inc=1, device_id={"sector": who},
                            device_id_type=pl.DeviceIdType.MESH)

    for x in range(1, TEAM):
        greet(line * TEAM + peer(x))

    @pl.when(line > 0)
    def _():
        greet(me - TEAM)

    @pl.when(line < lines - 1)
    def _():
        greet(me + TEAM)

    ends = (line == 0).astype(jnp.int32) + (line == lines - 1).astype(jnp.int32)
    pl.semaphore_wait(barrier, TEAM + 1 - ends)

    def remote(src, dst, send, recv, who):
        return pltpu.make_async_remote_copy(
            src_ref=src, dst_ref=dst, send_sem=send, recv_sem=recv,
            device_id={"sector": who}, device_id_type=pl.DeviceIdType.MESH)

    def team_copy(x, part):
        q = x * PARTS + part
        other = peer(x)
        return remote(right_ref.at[pl.ds(other * terms + part * half, half)],
                      right_all.at[me, pl.ds(part * half, half)],
                      team_send.at[q], team_recv.at[q], line * TEAM + other)

    def left_copy(x):
        other = peer(x)
        return remote(left_ref.at[pl.ds(other * terms, terms)], left_all.at[member],
                      side_send.at[0, x], side_recv.at[0, x], line * TEAM + other)

    def wave_copy(x):
        other = peer(x)
        return remote(wave_ref, wave_all.at[member],
                      side_send.at[1, x], side_recv.at[1, x], line * TEAM + other)

    def line_copy(up, hop, q):
        x, part = q // PARTS, q % PARTS
        step = 1 if up else -1
        origin = (line - step * (hop - 1)) * TEAM + peer(x)
        there = right_all.at[origin, pl.ds(part * half, half)]
        if hop == 1 and x == 0:
            src = right_ref.at[pl.ds(member * terms + part * half, half)]
        else:
            src = there
        side = 0 if up else 1
        return remote(src, there, line_send.at[side, hop - 1, q],
                      line_recv.at[side, hop - 1, q], me + step * TEAM)

    def can_send(up, hop):
        if up:
            return (line >= hop - 1) & (line < lines - 1)
        return (line + hop - 1 < lines) & (line > 0)

    keep = [
        pltpu.make_async_copy(right_ref.at[pl.ds(member * terms, terms)], right_all.at[me], local_sem.at[0]),
        pltpu.make_async_copy(left_ref.at[pl.ds(member * terms, terms)], left_all.at[member], local_sem.at[1]),
        pltpu.make_async_copy(wave_ref, wave_all.at[member], local_sem.at[2]),
    ]
    for q in range(PARTS, pieces):
        team_copy(q // PARTS, q % PARTS).start()
    for slot in range(pieces + lines - 2):
        for hop in range(1, lines):
            q = slot - (hop - 1)
            if not 0 <= q < pieces:
                continue
            if hop == 1 and q >= PARTS:
                team_copy(q // PARTS, q % PARTS).wait_recv()
            for up in (True, False):
                @pl.when(can_send(up, hop))
                def _():
                    if hop > 1:
                        line_copy(up, hop - 1, q).wait_recv()
                    line_copy(up, hop, q).start()
        if slot == PARTS - 1:
            for copy in keep:
                copy.start()
            for x in range(1, TEAM):
                left_copy(x).start()
                wave_copy(x).start()
    for q in range(pieces):
        for hop in range(1, lines):
            for up in (True, False):
                end = lines - 1 if up else 0
                from_there = (line >= hop) if up else (line + hop < lines)

                @pl.when((line == end) & from_there)
                def _():
                    line_copy(up, hop, q).wait_recv()

                @pl.when(can_send(up, hop))
                def _():
                    line_copy(up, hop, q).wait_send()
    for q in range(PARTS, pieces):
        team_copy(q // PARTS, q % PARTS).wait_send()
    for x in range(1, TEAM):
        left_copy(x).wait()
        wave_copy(x).wait()
    for copy in keep:
        copy.wait()


def exchange(wave, left_env, right_env, peer_count):
    total, sectors, size, _ = left_env.shape
    terms = total // TEAM
    lines = peer_count // TEAM
    pieces = TEAM * PARTS
    dma = pltpu.SemaphoreType.DMA
    hbm = pl.BlockSpec(memory_space=pl.ANY)
    return pl.pallas_call(
        functools.partial(exchange_kernel, lines, terms),
        out_shape=(
            jax.ShapeDtypeStruct((TEAM, terms, sectors, size, size), left_env.dtype),
            jax.ShapeDtypeStruct((peer_count, terms, sectors, size, size), right_env.dtype),
            jax.ShapeDtypeStruct((TEAM,) + wave.shape, wave.dtype),
        ),
        in_specs=[hbm] * 3,
        out_specs=(hbm, hbm, hbm),
        scratch_shapes=[
            dma((pieces,)), dma((pieces,)),
            dma((2, TEAM)), dma((2, TEAM)),
            dma((2, lines - 1, pieces)), dma((2, lines - 1, pieces)),
            dma((3,)),
        ],
        compiler_params=pltpu.CompilerParams(collective_id=0, has_side_effects=True),
        name="exchange",
    )(left_env, right_env, wave)


def products_kernel(partners, terms, pairs_ref, rows_ref, cols_ref, left_ref, wave_ref, *rest):
    right_refs, out_ref = rest[:partners], rest[partners]
    size = wave_ref.shape[-1]
    step = pl.program_id(0)
    row_ids = lax.broadcasted_iota(jnp.int32, (size, size), 0)
    col_ids = lax.broadcasted_iota(jnp.int32, (size, size), 1)
    masked = []
    for k in range(partners):
        live = (row_ids < rows_ref[step]) & (col_ids < cols_ref[step * partners + k])
        masked.append(jnp.where(live, wave_ref[0, 0, k], jnp.zeros((), wave_ref.dtype)))
    masked = jnp.concatenate(masked, axis=1)
    halves = [jnp.dot(left_ref[0, w, 0], masked, preferred_element_type=jnp.float32).astype(jnp.bfloat16)
              for w in range(terms)]
    for k in range(partners):
        first = jnp.concatenate([p[:, k * size:(k + 1) * size] for p in halves], axis=1)
        second = jnp.concatenate([right_refs[k][0, w, 0] for w in range(terms)], axis=1)
        out_ref[0, 0, k] = lax.dot_general(
            first, second, (((1,), (1,)), ((), ())), preferred_element_type=jnp.float32
        ).astype(out_ref.dtype)


def products(pairs, rows, cols, left_all, right_all, wave_all):
    team, sectors, partners, size, _ = wave_all.shape
    terms = left_all.shape[1]

    def pick(k):
        def index(i, pairs_ref, rows_ref, cols_ref):
            b = pairs_ref[i * partners + k]
            return (b // sectors, 0, b % sectors, 0, 0)
        return pl.BlockSpec((1, terms, 1, size, size), index)

    def own(i, *_):
        return (i // sectors, i % sectors, 0, 0, 0)

    blocks = team * sectors * partners
    return pl.pallas_call(
        functools.partial(products_kernel, partners, terms),
        grid_spec=pltpu.PrefetchScalarGridSpec(
            num_scalar_prefetch=3,
            grid=(team * sectors,),
            in_specs=[
                pl.BlockSpec((1, terms, 1, size, size), lambda i, *_: (i // sectors, 0, i % sectors, 0, 0)),
                pl.BlockSpec((1, 1, partners, size, size), own),
            ] + [pick(k) for k in range(partners)],
            out_specs=pl.BlockSpec((1, 1, partners, size, size), own),
        ),
        out_shape=jax.ShapeDtypeStruct(wave_all.shape, jnp.float32),
        compiler_params=pltpu.CompilerParams(vmem_limit_bytes=32 * 1024 * 1024),
        cost_estimate=pl.CostEstimate(flops=4 * blocks * terms * size ** 3,
                                      bytes_accessed=28 * 2 ** 20, transcendentals=0),
        name="products",
    )(pairs, rows, cols, left_all, wave_all, *([right_all] * partners))


def finish_kernel(peers, rows_ref, cols_ref, sums_ref, wave_ref, energy_ref, sigma_ref, correction_ref,
                  far_own, far_in, far_out, near_own, near_in, cross_in, mine, gathered,
                  load_sem, near_send, near_recv, far_send, far_recv, cross_send, cross_recv, stat_send, stat_recv):
    sectors, partners, size, _ = wave_ref.shape
    me = lax.axis_index("sector")
    line = me // TEAM
    member = me % TEAM
    row, core = member // 2, member % 2
    near = line * TEAM + row * 2 + 1 - core
    cross = line * TEAM + (1 - row) * 2 + core

    barrier = pltpu.get_barrier_semaphore()

    @pl.loop(1, peers)
    def _(d):
        pl.semaphore_signal(barrier, inc=1, device_id={"sector": lax.rem(me + d, peers)},
                            device_id_type=pl.DeviceIdType.MESH)

    pl.semaphore_wait(barrier, peers - 1)

    def remote(src, dst, send, recv, who):
        return pltpu.make_async_remote_copy(
            src_ref=src, dst_ref=dst, send_sem=send, recv_sem=recv,
            device_id={"sector": who}, device_id_type=pl.DeviceIdType.MESH)

    def far_copy(i):
        return remote(sums_ref.at[(1 - row) * 2 + 1 - core, i], far_in.at[i], far_send.at[i], far_recv.at[i], near)

    def near_copy(i):
        return remote(sums_ref.at[row * 2 + 1 - core, i], near_in.at[i], near_send.at[i], near_recv.at[i], near)

    def cross_copy(i):
        return remote(far_out.at[i], cross_in.at[i], cross_send.at[i], cross_recv.at[i], cross)

    def stat_copy(d):
        return remote(mine, gathered.at[me], stat_send.at[d], stat_recv.at[d], lax.rem(me + d, peers))

    load_far = pltpu.make_async_copy(sums_ref.at[(1 - row) * 2 + core], far_own, load_sem.at[0])
    load_near = pltpu.make_async_copy(sums_ref.at[member], near_own, load_sem.at[1])
    load_far.start()

    @pl.loop(0, sectors)
    def _(i):
        far_copy(i).start()

    load_near.start()

    @pl.loop(0, sectors)
    def _(i):
        near_copy(i).start()

    load_far.wait()

    @pl.loop(0, sectors)
    def _(i):
        far_copy(i).wait_recv()
        far_out[i] = (far_own[i] + far_in[i]).astype(far_out.dtype)
        cross_copy(i).start()

    load_near.wait()
    row_ids = lax.broadcasted_iota(jnp.int32, (size, size), 0)
    col_ids = lax.broadcasted_iota(jnp.int32, (size, size), 1)

    def fold(x):
        return jnp.sum(x.reshape(size // 8, 8, size), axis=0)

    mine[...] = jnp.zeros_like(mine)

    @pl.loop(0, sectors)
    def _(i):
        near_copy(i).wait_recv()
        cross_copy(i).wait_recv()
        for k in range(partners):
            live = (row_ids < rows_ref[i]) & (col_ids < cols_ref[i * partners + k])
            masked = jnp.where(live, wave_ref[i, k].astype(jnp.float32), 0.0)
            total = near_own[i, k] + near_in[i, k] + cross_in[i, k].astype(jnp.float32)
            sigma = jnp.where(live, total, 0.0).astype(jnp.bfloat16)
            sigma_ref[i, k] = sigma
            mine[0:8] += fold(masked * sigma.astype(jnp.float32))
            mine[8:16] += fold(masked * masked)

    @pl.loop(1, peers)
    def _(d):
        stat_copy(d).start()

    gathered[me] = mine[...]

    @pl.loop(0, sectors)
    def _(i):
        far_copy(i).wait_send()
        near_copy(i).wait_send()
        cross_copy(i).wait_send()

    @pl.loop(1, peers)
    def _(d):
        stat_copy(d).wait()

    both = jnp.sum(gathered[...], axis=0)
    correlation = jnp.sum(jnp.sum(both[0:8], axis=0, keepdims=True), axis=1, keepdims=True)
    norm_sum = jnp.sum(jnp.sum(both[8:16], axis=0, keepdims=True), axis=1, keepdims=True)
    quotient = correlation / norm_sum

    @pl.loop(0, sectors)
    def _(i):
        for k in range(partners):
            live = (row_ids < rows_ref[i]) & (col_ids < cols_ref[i * partners + k])
            masked = jnp.where(live, wave_ref[i, k].astype(jnp.float32), 0.0)
            residual = sigma_ref[i, k].astype(jnp.float32) - quotient * masked
            distance = quotient - energy_ref[i, k]
            correction_ref[i, k] = residual * distance / (distance * distance + 0.25)


def finish(rows, cols, sums, wave, energy, peers):
    sectors, partners, size, _ = wave.shape
    dma = pltpu.SemaphoreType.DMA
    smem = pl.BlockSpec(memory_space=pltpu.SMEM)
    vmem = pl.BlockSpec(memory_space=pltpu.VMEM)
    return pl.pallas_call(
        functools.partial(finish_kernel, peers),
        out_shape=(
            jax.ShapeDtypeStruct(wave.shape, jnp.bfloat16),
            jax.ShapeDtypeStruct(wave.shape, jnp.float32),
        ),
        in_specs=[smem, smem, pl.BlockSpec(memory_space=pl.ANY), vmem, vmem],
        out_specs=(vmem, vmem),
        scratch_shapes=[
            pltpu.VMEM(wave.shape, jnp.float32), pltpu.VMEM(wave.shape, jnp.float32),
            pltpu.VMEM(wave.shape, jnp.bfloat16),
            pltpu.VMEM(wave.shape, jnp.float32), pltpu.VMEM(wave.shape, jnp.float32),
            pltpu.VMEM(wave.shape, jnp.bfloat16),
            pltpu.VMEM((16, size), jnp.float32), pltpu.VMEM((peers, 16, size), jnp.float32),
            dma((2,)), dma((sectors,)), dma((sectors,)), dma((sectors,)), dma((sectors,)),
            dma((sectors,)), dma((sectors,)), dma((peers,)), dma((peers,)),
        ],
        compiler_params=pltpu.CompilerParams(collective_id=1, has_side_effects=True,
                                             vmem_limit_bytes=40 * 1024 * 1024),
        name="finish",
    )(rows, cols, sums, wave, energy)


def body(wavefunction, left_env, right_env, energy_diag, sector_dims, pair_table):
    local_sectors = wavefunction.shape[0]
    peer_count = lax.axis_size("sector")
    my_index = lax.axis_index("sector")
    line = my_index // TEAM
    team_sectors = TEAM * local_sectors
    team_first = line * team_sectors
    team_pairs = lax.dynamic_slice_in_dim(pair_table, team_first, team_sectors, 0)
    team_rows = lax.dynamic_slice_in_dim(sector_dims[0], team_first, team_sectors, 0)
    team_cols = jnp.take(sector_dims[1], team_pairs)
    left_all, right_all, wave_all = exchange(wavefunction, left_env, right_env, peer_count)
    sums = products(team_pairs.reshape(-1), team_rows, team_cols.reshape(-1), left_all, right_all, wave_all)
    member_first = (my_index % TEAM) * local_sectors
    rows = lax.dynamic_slice_in_dim(team_rows, member_first, local_sectors, 0)
    cols = lax.dynamic_slice_in_dim(team_cols, member_first, local_sectors, 0)
    return finish(rows, cols.reshape(-1), sums, wavefunction, energy_diag, peer_count)


def solution(mesh):
    blocks = P(("groups", "sector"), None, None, None)
    environments = P(None, ("groups", "sector"), None, None)
    return jax.shard_map(
        body,
        mesh=mesh,
        in_specs=(blocks, environments, environments, blocks, P(), P()),
        out_specs=(blocks, blocks),
        check_vma=False,
    )
```

```python
import functools
import jax
import jax.numpy as jnp
from jax import lax
from jax.experimental import pallas as pl
from jax.experimental.pallas import tpu as pltpu
from jax.sharding import PartitionSpec as P

TEAM = 4
PARTS = 2


def exchange_kernel(lines, terms, left_ref, right_ref, wave_ref, left_all, right_all, wave_all,
                    team_send, team_recv, side_send, side_recv, line_send, line_recv, local_sem):
    me = lax.axis_index("sector")
    line = me // TEAM
    member = me % TEAM
    half = terms // PARTS
    pieces = TEAM * PARTS

    def peer(x):
        return ((member // 2 + x // 2) % 2) * 2 + (member % 2 + x % 2) % 2

    barrier = pltpu.get_barrier_semaphore()

    def greet(who):
        pl.semaphore_signal(barrier, inc=1, device_id={"sector": who},
                            device_id_type=pl.DeviceIdType.MESH)

    for x in range(1, TEAM):
        greet(line * TEAM + peer(x))

    @pl.when(line > 0)
    def _():
        greet(me - TEAM)

    @pl.when(line < lines - 1)
    def _():
        greet(me + TEAM)

    ends = (line == 0).astype(jnp.int32) + (line == lines - 1).astype(jnp.int32)
    pl.semaphore_wait(barrier, TEAM + 1 - ends)

    def remote(src, dst, send, recv, who):
        return pltpu.make_async_remote_copy(
            src_ref=src, dst_ref=dst, send_sem=send, recv_sem=recv,
            device_id={"sector": who}, device_id_type=pl.DeviceIdType.MESH)

    def team_copy(x, part):
        q = x * PARTS + part
        other = peer(x)
        return remote(right_ref.at[pl.ds(other * terms + part * half, half)],
                      right_all.at[me, pl.ds(part * half, half)],
                      team_send.at[q], team_recv.at[q], line * TEAM + other)

    def left_copy(x):
        other = peer(x)
        return remote(left_ref.at[pl.ds(other * terms, terms)], left_all.at[member],
                      side_send.at[0, x], side_recv.at[0, x], line * TEAM + other)

    def wave_copy(x):
        other = peer(x)
        return remote(wave_ref, wave_all.at[member],
                      side_send.at[1, x], side_recv.at[1, x], line * TEAM + other)

    def line_copy(up, hop, q):
        x, part = q // PARTS, q % PARTS
        step = 1 if up else -1
        origin = (line - step * (hop - 1)) * TEAM + peer(x)
        there = right_all.at[origin, pl.ds(part * half, half)]
        if hop == 1 and x == 0:
            src = right_ref.at[pl.ds(member * terms + part * half, half)]
        else:
            src = there
        side = 0 if up else 1
        return remote(src, there, line_send.at[side, hop - 1, q],
                      line_recv.at[side, hop - 1, q], me + step * TEAM)

    def can_send(up, hop):
        if up:
            return (line >= hop - 1) & (line < lines - 1)
        return (line + hop - 1 < lines) & (line > 0)

    keep = [
        pltpu.make_async_copy(right_ref.at[pl.ds(member * terms, terms)], right_all.at[me], local_sem.at[0]),
        pltpu.make_async_copy(left_ref.at[pl.ds(member * terms, terms)], left_all.at[member], local_sem.at[1]),
        pltpu.make_async_copy(wave_ref, wave_all.at[member], local_sem.at[2]),
    ]
    for q in range(PARTS, pieces):
        team_copy(q // PARTS, q % PARTS).start()
    for slot in range(pieces + lines - 2):
        for hop in range(1, lines):
            q = slot - (hop - 1)
            if not 0 <= q < pieces:
                continue
            if hop == 1 and q >= PARTS:
                team_copy(q // PARTS, q % PARTS).wait_recv()
            for up in (True, False):
                @pl.when(can_send(up, hop))
                def _():
                    if hop > 1:
                        line_copy(up, hop - 1, q).wait_recv()
                    line_copy(up, hop, q).start()
        if slot == PARTS - 1:
            for copy in keep:
                copy.start()
            for x in range(1, TEAM):
                left_copy(x).start()
                wave_copy(x).start()
    for q in range(pieces):
        for hop in range(1, lines):
            for up in (True, False):
                end = lines - 1 if up else 0
                from_there = (line >= hop) if up else (line + hop < lines)

                @pl.when((line == end) & from_there)
                def _():
                    line_copy(up, hop, q).wait_recv()

                @pl.when(can_send(up, hop))
                def _():
                    line_copy(up, hop, q).wait_send()
    for q in range(PARTS, pieces):
        team_copy(q // PARTS, q % PARTS).wait_send()
    for x in range(1, TEAM):
        left_copy(x).wait()
        wave_copy(x).wait()
    for copy in keep:
        copy.wait()


def exchange(wave, left_env, right_env, peer_count):
    total, sectors, size, _ = left_env.shape
    terms = total // TEAM
    lines = peer_count // TEAM
    pieces = TEAM * PARTS
    dma = pltpu.SemaphoreType.DMA
    hbm = pl.BlockSpec(memory_space=pl.ANY)
    return pl.pallas_call(
        functools.partial(exchange_kernel, lines, terms),
        out_shape=(
            jax.ShapeDtypeStruct((TEAM, terms, sectors, size, size), left_env.dtype),
            jax.ShapeDtypeStruct((peer_count, terms, sectors, size, size), right_env.dtype),
            jax.ShapeDtypeStruct((TEAM,) + wave.shape, wave.dtype),
        ),
        in_specs=[hbm] * 3,
        out_specs=(hbm, hbm, hbm),
        scratch_shapes=[
            dma((pieces,)), dma((pieces,)),
            dma((2, TEAM)), dma((2, TEAM)),
            dma((2, lines - 1, pieces)), dma((2, lines - 1, pieces)),
            dma((3,)),
        ],
        compiler_params=pltpu.CompilerParams(collective_id=0, has_side_effects=True),
        name="exchange",
    )(left_env, right_env, wave)


GROUP = 4


def products_kernel(group, partners, terms, pairs_ref, rows_ref, cols_ref, left_ref, wave_ref, *rest):
    right_refs, out_ref = rest[:group * partners], rest[group * partners]
    size = wave_ref.shape[-1]
    step = pl.program_id(0)
    row_ids = lax.broadcasted_iota(jnp.int32, (size, size), 0)
    col_ids = lax.broadcasted_iota(jnp.int32, (size, size), 1)
    for g in range(group):
        sector = step * group + g
        masked = []
        for k in range(partners):
            live = (row_ids < rows_ref[sector]) & (col_ids < cols_ref[sector * partners + k])
            masked.append(jnp.where(live, wave_ref[0, g, k], jnp.zeros((), wave_ref.dtype)))
        masked = jnp.concatenate(masked, axis=1)
        left = left_ref[0, :, g].reshape(terms * size, size)
        halves = jnp.dot(left, masked, preferred_element_type=jnp.float32).astype(jnp.bfloat16)
        for k in range(partners):
            first = jnp.concatenate(
                [halves[w * size:(w + 1) * size, k * size:(k + 1) * size] for w in range(terms)], axis=1)
            second = jnp.concatenate([right_refs[g * partners + k][0, w, 0] for w in range(terms)], axis=1)
            out_ref[0, g, k] = lax.dot_general(
                first, second, (((1,), (1,)), ((), ())), preferred_element_type=jnp.float32)


def products(pairs, rows, cols, left_all, right_all, wave_all):
    team, sectors, partners, size, _ = wave_all.shape
    terms = left_all.shape[1]
    group = GROUP if sectors % GROUP == 0 else 1
    steps = sectors // group

    def pick(g, k):
        def index(i, pairs_ref, rows_ref, cols_ref):
            b = pairs_ref[(i * group + g) * partners + k]
            return (b // sectors, 0, b % sectors, 0, 0)
        return pl.BlockSpec((1, terms, 1, size, size), index)

    def own(i, *_):
        return (i // steps, i % steps, 0, 0, 0)

    blocks = team * sectors * partners
    return pl.pallas_call(
        functools.partial(products_kernel, group, partners, terms),
        grid_spec=pltpu.PrefetchScalarGridSpec(
            num_scalar_prefetch=3,
            grid=(team * steps,),
            in_specs=[
                pl.BlockSpec((1, terms, group, size, size), lambda i, *_: (i // steps, 0, i % steps, 0, 0)),
                pl.BlockSpec((1, group, partners, size, size), own),
            ] + [pick(g, k) for g in range(group) for k in range(partners)],
            out_specs=pl.BlockSpec((1, group, partners, size, size), own),
        ),
        out_shape=jax.ShapeDtypeStruct(wave_all.shape, jnp.float32),
        compiler_params=pltpu.CompilerParams(vmem_limit_bytes=40 * 1024 * 1024),
        cost_estimate=pl.CostEstimate(flops=4 * blocks * terms * size ** 3,
                                      bytes_accessed=32 * 2 ** 20, transcendentals=0),
        name="products",
    )(pairs, rows, cols, left_all, wave_all, *([right_all] * (group * partners)))


def finish_kernel(peers, rows_ref, cols_ref, sums_ref, wave_ref, energy_ref, sigma_ref, correction_ref,
                  far_own, far_in, far_out, near_own, near_in, cross_in, mine, gathered,
                  load_sem, near_send, near_recv, far_send, far_recv, cross_send, cross_recv, stat_send, stat_recv):
    sectors, partners, size, _ = wave_ref.shape
    me = lax.axis_index("sector")
    line = me // TEAM
    member = me % TEAM
    row, core = member // 2, member % 2
    near = line * TEAM + row * 2 + 1 - core
    cross = line * TEAM + (1 - row) * 2 + core

    barrier = pltpu.get_barrier_semaphore()

    @pl.loop(1, peers)
    def _(d):
        pl.semaphore_signal(barrier, inc=1, device_id={"sector": lax.rem(me + d, peers)},
                            device_id_type=pl.DeviceIdType.MESH)

    pl.semaphore_wait(barrier, peers - 1)

    def remote(src, dst, send, recv, who):
        return pltpu.make_async_remote_copy(
            src_ref=src, dst_ref=dst, send_sem=send, recv_sem=recv,
            device_id={"sector": who}, device_id_type=pl.DeviceIdType.MESH)

    def far_copy(i):
        return remote(sums_ref.at[(1 - row) * 2 + 1 - core, i], far_in.at[i], far_send.at[i], far_recv.at[i], near)

    def near_copy(i):
        return remote(sums_ref.at[row * 2 + 1 - core, i], near_in.at[i], near_send.at[i], near_recv.at[i], near)

    def cross_copy(i):
        return remote(far_out.at[i], cross_in.at[i], cross_send.at[i], cross_recv.at[i], cross)

    def stat_copy(d):
        return remote(mine, gathered.at[me], stat_send.at[d], stat_recv.at[d], lax.rem(me + d, peers))

    load_far = pltpu.make_async_copy(sums_ref.at[(1 - row) * 2 + core], far_own, load_sem.at[0])
    load_near = pltpu.make_async_copy(sums_ref.at[member], near_own, load_sem.at[1])
    load_far.start()

    @pl.loop(0, sectors)
    def _(i):
        far_copy(i).start()

    load_near.start()

    @pl.loop(0, sectors)
    def _(i):
        near_copy(i).start()

    load_far.wait()

    @pl.loop(0, sectors)
    def _(i):
        far_copy(i).wait_recv()
        far_out[i] = (far_own[i] + far_in[i]).astype(far_out.dtype)
        cross_copy(i).start()

    load_near.wait()
    row_ids = lax.broadcasted_iota(jnp.int32, (size, size), 0)
    col_ids = lax.broadcasted_iota(jnp.int32, (size, size), 1)

    def fold(x):
        return jnp.sum(x.reshape(size // 8, 8, size), axis=0)

    mine[...] = jnp.zeros_like(mine)

    @pl.loop(0, sectors)
    def _(i):
        near_copy(i).wait_recv()
        cross_copy(i).wait_recv()
        for k in range(partners):
            live = (row_ids < rows_ref[i]) & (col_ids < cols_ref[i * partners + k])
            masked = jnp.where(live, wave_ref[i, k].astype(jnp.float32), 0.0)
            total = near_own[i, k] + near_in[i, k] + cross_in[i, k].astype(jnp.float32)
            sigma = jnp.where(live, total, 0.0).astype(jnp.bfloat16)
            sigma_ref[i, k] = sigma
            mine[0:8] += fold(masked * sigma.astype(jnp.float32))
            mine[8:16] += fold(masked * masked)

    @pl.loop(1, peers)
    def _(d):
        stat_copy(d).start()

    gathered[me] = mine[...]

    @pl.loop(0, sectors)
    def _(i):
        far_copy(i).wait_send()
        near_copy(i).wait_send()
        cross_copy(i).wait_send()

    @pl.loop(1, peers)
    def _(d):
        stat_copy(d).wait()

    both = jnp.sum(gathered[...], axis=0)
    correlation = jnp.sum(jnp.sum(both[0:8], axis=0, keepdims=True), axis=1, keepdims=True)
    norm_sum = jnp.sum(jnp.sum(both[8:16], axis=0, keepdims=True), axis=1, keepdims=True)
    quotient = correlation / norm_sum

    @pl.loop(0, sectors)
    def _(i):
        for k in range(partners):
            live = (row_ids < rows_ref[i]) & (col_ids < cols_ref[i * partners + k])
            masked = jnp.where(live, wave_ref[i, k].astype(jnp.float32), 0.0)
            residual = sigma_ref[i, k].astype(jnp.float32) - quotient * masked
            distance = quotient - energy_ref[i, k]
            correction_ref[i, k] = residual * distance / (distance * distance + 0.25)


def finish(rows, cols, sums, wave, energy, peers):
    sectors, partners, size, _ = wave.shape
    dma = pltpu.SemaphoreType.DMA
    smem = pl.BlockSpec(memory_space=pltpu.SMEM)
    vmem = pl.BlockSpec(memory_space=pltpu.VMEM)
    return pl.pallas_call(
        functools.partial(finish_kernel, peers),
        out_shape=(
            jax.ShapeDtypeStruct(wave.shape, jnp.bfloat16),
            jax.ShapeDtypeStruct(wave.shape, jnp.float32),
        ),
        in_specs=[smem, smem, pl.BlockSpec(memory_space=pl.ANY), vmem, vmem],
        out_specs=(vmem, vmem),
        scratch_shapes=[
            pltpu.VMEM(wave.shape, jnp.float32), pltpu.VMEM(wave.shape, jnp.float32),
            pltpu.VMEM(wave.shape, jnp.bfloat16),
            pltpu.VMEM(wave.shape, jnp.float32), pltpu.VMEM(wave.shape, jnp.float32),
            pltpu.VMEM(wave.shape, jnp.bfloat16),
            pltpu.VMEM((16, size), jnp.float32), pltpu.VMEM((peers, 16, size), jnp.float32),
            dma((2,)), dma((sectors,)), dma((sectors,)), dma((sectors,)), dma((sectors,)),
            dma((sectors,)), dma((sectors,)), dma((peers,)), dma((peers,)),
        ],
        compiler_params=pltpu.CompilerParams(collective_id=1, has_side_effects=True,
                                             vmem_limit_bytes=40 * 1024 * 1024),
        name="finish",
    )(rows, cols, sums, wave, energy)


def body(wavefunction, left_env, right_env, energy_diag, sector_dims, pair_table):
    local_sectors = wavefunction.shape[0]
    peer_count = lax.axis_size("sector")
    my_index = lax.axis_index("sector")
    line = my_index // TEAM
    team_sectors = TEAM * local_sectors
    team_first = line * team_sectors
    team_pairs = lax.dynamic_slice_in_dim(pair_table, team_first, team_sectors, 0)
    team_rows = lax.dynamic_slice_in_dim(sector_dims[0], team_first, team_sectors, 0)
    team_cols = jnp.take(sector_dims[1], team_pairs)
    left_all, right_all, wave_all = exchange(wavefunction, left_env, right_env, peer_count)
    sums = products(team_pairs.reshape(-1), team_rows, team_cols.reshape(-1), left_all, right_all, wave_all)
    member_first = (my_index % TEAM) * local_sectors
    rows = lax.dynamic_slice_in_dim(team_rows, member_first, local_sectors, 0)
    cols = lax.dynamic_slice_in_dim(team_cols, member_first, local_sectors, 0)
    return finish(rows, cols.reshape(-1), sums, wavefunction, energy_diag, peer_count)


def solution(mesh):
    blocks = P(("groups", "sector"), None, None, None)
    environments = P(None, ("groups", "sector"), None, None)
    return jax.shard_map(
        body,
        mesh=mesh,
        in_specs=(blocks, environments, environments, blocks, P(), P()),
        out_specs=(blocks, blocks),
        check_vma=False,
    )
```

```python
import functools
import jax
import jax.numpy as jnp
from jax import lax
from jax.experimental import pallas as pl
from jax.experimental.pallas import tpu as pltpu
from jax.sharding import PartitionSpec as P

TEAM = 4
PARTS = 4


def exchange_kernel(lines, terms, left_ref, right_ref, wave_ref, left_all, right_all, wave_all,
                    team_send, team_recv, side_send, side_recv, line_send, line_recv, local_sem):
    me = lax.axis_index("sector")
    line = me // TEAM
    member = me % TEAM
    half = terms // PARTS
    pieces = TEAM * PARTS

    def peer(x):
        return ((member // 2 + x // 2) % 2) * 2 + (member % 2 + x % 2) % 2

    barrier = pltpu.get_barrier_semaphore()

    def greet(who):
        pl.semaphore_signal(barrier, inc=1, device_id={"sector": who},
                            device_id_type=pl.DeviceIdType.MESH)

    for x in range(1, TEAM):
        greet(line * TEAM + peer(x))

    @pl.when(line > 0)
    def _():
        greet(me - TEAM)

    @pl.when(line < lines - 1)
    def _():
        greet(me + TEAM)

    ends = (line == 0).astype(jnp.int32) + (line == lines - 1).astype(jnp.int32)
    pl.semaphore_wait(barrier, TEAM + 1 - ends)

    def remote(src, dst, send, recv, who):
        return pltpu.make_async_remote_copy(
            src_ref=src, dst_ref=dst, send_sem=send, recv_sem=recv,
            device_id={"sector": who}, device_id_type=pl.DeviceIdType.MESH)

    def team_copy(x, part):
        q = x * PARTS + part
        other = peer(x)
        return remote(right_ref.at[pl.ds(other * terms + part * half, half)],
                      right_all.at[me, pl.ds(part * half, half)],
                      team_send.at[q], team_recv.at[q], line * TEAM + other)

    def left_copy(x):
        other = peer(x)
        return remote(left_ref.at[pl.ds(other * terms, terms)], left_all.at[member],
                      side_send.at[0, x], side_recv.at[0, x], line * TEAM + other)

    def wave_copy(x):
        other = peer(x)
        return remote(wave_ref, wave_all.at[member],
                      side_send.at[1, x], side_recv.at[1, x], line * TEAM + other)

    def line_copy(up, hop, q):
        x, part = q // PARTS, q % PARTS
        step = 1 if up else -1
        origin = (line - step * (hop - 1)) * TEAM + peer(x)
        there = right_all.at[origin, pl.ds(part * half, half)]
        if hop == 1 and x == 0:
            src = right_ref.at[pl.ds(member * terms + part * half, half)]
        else:
            src = there
        side = 0 if up else 1
        return remote(src, there, line_send.at[side, hop - 1, q],
                      line_recv.at[side, hop - 1, q], me + step * TEAM)

    def can_send(up, hop):
        if up:
            return (line >= hop - 1) & (line < lines - 1)
        return (line + hop - 1 < lines) & (line > 0)

    keep = [
        pltpu.make_async_copy(right_ref.at[pl.ds(member * terms, terms)], right_all.at[me], local_sem.at[0]),
        pltpu.make_async_copy(left_ref.at[pl.ds(member * terms, terms)], left_all.at[member], local_sem.at[1]),
        pltpu.make_async_copy(wave_ref, wave_all.at[member], local_sem.at[2]),
    ]
    for q in range(PARTS, pieces):
        team_copy(q // PARTS, q % PARTS).start()
    for slot in range(pieces + lines - 2):
        for hop in range(1, lines):
            q = slot - (hop - 1)
            if not 0 <= q < pieces:
                continue
            if hop == 1 and q >= PARTS:
                team_copy(q // PARTS, q % PARTS).wait_recv()
            for up in (True, False):
                @pl.when(can_send(up, hop))
                def _():
                    if hop > 1:
                        line_copy(up, hop - 1, q).wait_recv()
                    line_copy(up, hop, q).start()
        if slot == PARTS - 1:
            for copy in keep:
                copy.start()
            for x in range(1, TEAM):
                left_copy(x).start()
                wave_copy(x).start()
    for q in range(pieces):
        for hop in range(1, lines):
            for up in (True, False):
                end = lines - 1 if up else 0
                from_there = (line >= hop) if up else (line + hop < lines)

                @pl.when((line == end) & from_there)
                def _():
                    line_copy(up, hop, q).wait_recv()

                @pl.when(can_send(up, hop))
                def _():
                    line_copy(up, hop, q).wait_send()
    for q in range(PARTS, pieces):
        team_copy(q // PARTS, q % PARTS).wait_send()
    for x in range(1, TEAM):
        left_copy(x).wait()
        wave_copy(x).wait()
    for copy in keep:
        copy.wait()


def exchange(wave, left_env, right_env, peer_count):
    total, sectors, size, _ = left_env.shape
    terms = total // TEAM
    lines = peer_count // TEAM
    pieces = TEAM * PARTS
    dma = pltpu.SemaphoreType.DMA
    hbm = pl.BlockSpec(memory_space=pl.ANY)
    return pl.pallas_call(
        functools.partial(exchange_kernel, lines, terms),
        out_shape=(
            jax.ShapeDtypeStruct((TEAM, terms, sectors, size, size), left_env.dtype),
            jax.ShapeDtypeStruct((peer_count, terms, sectors, size, size), right_env.dtype),
            jax.ShapeDtypeStruct((TEAM,) + wave.shape, wave.dtype),
        ),
        in_specs=[hbm] * 3,
        out_specs=(hbm, hbm, hbm),
        scratch_shapes=[
            dma((pieces,)), dma((pieces,)),
            dma((2, TEAM)), dma((2, TEAM)),
            dma((2, lines - 1, pieces)), dma((2, lines - 1, pieces)),
            dma((3,)),
        ],
        compiler_params=pltpu.CompilerParams(collective_id=0, has_side_effects=True),
        name="exchange",
    )(left_env, right_env, wave)


GROUP = 4


def products_kernel(group, partners, terms, pairs_ref, rows_ref, cols_ref, left_ref, wave_ref, *rest):
    right_refs, out_ref = rest[:group * partners], rest[group * partners]
    size = wave_ref.shape[-1]
    step = pl.program_id(0)
    row_ids = lax.broadcasted_iota(jnp.int32, (size, size), 0)
    col_ids = lax.broadcasted_iota(jnp.int32, (size, size), 1)
    for g in range(group):
        sector = step * group + g
        masked = []
        for k in range(partners):
            live = (row_ids < rows_ref[sector]) & (col_ids < cols_ref[sector * partners + k])
            masked.append(jnp.where(live, wave_ref[0, g, k], jnp.zeros((), wave_ref.dtype)))
        masked = jnp.concatenate(masked, axis=1)
        left = left_ref[0, :, g].reshape(terms * size, size)
        halves = jnp.dot(left, masked, preferred_element_type=jnp.float32).astype(jnp.bfloat16)
        for k in range(partners):
            first = jnp.concatenate(
                [halves[w * size:(w + 1) * size, k * size:(k + 1) * size] for w in range(terms)], axis=1)
            second = jnp.concatenate([right_refs[g * partners + k][0, w, 0] for w in range(terms)], axis=1)
            out_ref[0, g, k] = lax.dot_general(
                first, second, (((1,), (1,)), ((), ())), preferred_element_type=jnp.float32)


def products(pairs, rows, cols, left_all, right_all, wave_all):
    team, sectors, partners, size, _ = wave_all.shape
    terms = left_all.shape[1]
    group = GROUP if sectors % GROUP == 0 else 1
    steps = sectors // group

    def pick(g, k):
        def index(i, pairs_ref, rows_ref, cols_ref):
            b = pairs_ref[(i * group + g) * partners + k]
            return (b // sectors, 0, b % sectors, 0, 0)
        return pl.BlockSpec((1, terms, 1, size, size), index)

    def own(i, *_):
        return (i // steps, i % steps, 0, 0, 0)

    blocks = team * sectors * partners
    return pl.pallas_call(
        functools.partial(products_kernel, group, partners, terms),
        grid_spec=pltpu.PrefetchScalarGridSpec(
            num_scalar_prefetch=3,
            grid=(team * steps,),
            in_specs=[
                pl.BlockSpec((1, terms, group, size, size), lambda i, *_: (i // steps, 0, i % steps, 0, 0)),
                pl.BlockSpec((1, group, partners, size, size), own),
            ] + [pick(g, k) for g in range(group) for k in range(partners)],
            out_specs=pl.BlockSpec((1, group, partners, size, size), own),
        ),
        out_shape=jax.ShapeDtypeStruct(wave_all.shape, jnp.float32),
        compiler_params=pltpu.CompilerParams(vmem_limit_bytes=40 * 1024 * 1024),
        cost_estimate=pl.CostEstimate(flops=4 * blocks * terms * size ** 3,
                                      bytes_accessed=32 * 2 ** 20, transcendentals=0),
        name="products",
    )(pairs, rows, cols, left_all, wave_all, *([right_all] * (group * partners)))


def finish_kernel(peers, rows_ref, cols_ref, sums_ref, wave_ref, energy_ref, sigma_ref, correction_ref,
                  far_own, far_in, far_out, near_own, near_in, cross_in, mine, gathered,
                  load_sem, near_send, near_recv, far_send, far_recv, cross_send, cross_recv, stat_send, stat_recv):
    sectors, partners, size, _ = wave_ref.shape
    me = lax.axis_index("sector")
    line = me // TEAM
    member = me % TEAM
    row, core = member // 2, member % 2
    near = line * TEAM + row * 2 + 1 - core
    cross = line * TEAM + (1 - row) * 2 + core

    barrier = pltpu.get_barrier_semaphore()

    @pl.loop(1, peers)
    def _(d):
        pl.semaphore_signal(barrier, inc=1, device_id={"sector": lax.rem(me + d, peers)},
                            device_id_type=pl.DeviceIdType.MESH)

    pl.semaphore_wait(barrier, peers - 1)

    def remote(src, dst, send, recv, who):
        return pltpu.make_async_remote_copy(
            src_ref=src, dst_ref=dst, send_sem=send, recv_sem=recv,
            device_id={"sector": who}, device_id_type=pl.DeviceIdType.MESH)

    def far_copy(i):
        return remote(sums_ref.at[(1 - row) * 2 + 1 - core, i], far_in.at[i], far_send.at[i], far_recv.at[i], near)

    def near_copy(i):
        return remote(sums_ref.at[row * 2 + 1 - core, i], near_in.at[i], near_send.at[i], near_recv.at[i], near)

    def cross_copy(i):
        return remote(far_out.at[i], cross_in.at[i], cross_send.at[i], cross_recv.at[i], cross)

    def stat_copy(d):
        return remote(mine, gathered.at[me], stat_send.at[d], stat_recv.at[d], lax.rem(me + d, peers))

    load_far = pltpu.make_async_copy(sums_ref.at[(1 - row) * 2 + core], far_own, load_sem.at[0])
    load_near = pltpu.make_async_copy(sums_ref.at[member], near_own, load_sem.at[1])
    load_far.start()

    @pl.loop(0, sectors)
    def _(i):
        far_copy(i).start()

    load_near.start()

    @pl.loop(0, sectors)
    def _(i):
        near_copy(i).start()

    load_far.wait()

    @pl.loop(0, sectors)
    def _(i):
        far_copy(i).wait_recv()
        far_out[i] = (far_own[i] + far_in[i]).astype(far_out.dtype)
        cross_copy(i).start()

    load_near.wait()
    row_ids = lax.broadcasted_iota(jnp.int32, (size, size), 0)
    col_ids = lax.broadcasted_iota(jnp.int32, (size, size), 1)

    def fold(x):
        return jnp.sum(x.reshape(size // 8, 8, size), axis=0)

    mine[...] = jnp.zeros_like(mine)

    @pl.loop(0, sectors)
    def _(i):
        near_copy(i).wait_recv()
        cross_copy(i).wait_recv()
        for k in range(partners):
            live = (row_ids < rows_ref[i]) & (col_ids < cols_ref[i * partners + k])
            masked = jnp.where(live, wave_ref[i, k].astype(jnp.float32), 0.0)
            total = near_own[i, k] + near_in[i, k] + cross_in[i, k].astype(jnp.float32)
            sigma = jnp.where(live, total, 0.0).astype(jnp.bfloat16)
            sigma_ref[i, k] = sigma
            mine[0:8] += fold(masked * sigma.astype(jnp.float32))
            mine[8:16] += fold(masked * masked)

    @pl.loop(1, peers)
    def _(d):
        stat_copy(d).start()

    gathered[me] = mine[...]

    @pl.loop(0, sectors)
    def _(i):
        far_copy(i).wait_send()
        near_copy(i).wait_send()
        cross_copy(i).wait_send()

    @pl.loop(1, peers)
    def _(d):
        stat_copy(d).wait()

    both = jnp.sum(gathered[...], axis=0)
    correlation = jnp.sum(jnp.sum(both[0:8], axis=0, keepdims=True), axis=1, keepdims=True)
    norm_sum = jnp.sum(jnp.sum(both[8:16], axis=0, keepdims=True), axis=1, keepdims=True)
    quotient = correlation / norm_sum

    @pl.loop(0, sectors)
    def _(i):
        for k in range(partners):
            live = (row_ids < rows_ref[i]) & (col_ids < cols_ref[i * partners + k])
            masked = jnp.where(live, wave_ref[i, k].astype(jnp.float32), 0.0)
            residual = sigma_ref[i, k].astype(jnp.float32) - quotient * masked
            distance = quotient - energy_ref[i, k]
            correction_ref[i, k] = residual * distance / (distance * distance + 0.25)


def finish(rows, cols, sums, wave, energy, peers):
    sectors, partners, size, _ = wave.shape
    dma = pltpu.SemaphoreType.DMA
    smem = pl.BlockSpec(memory_space=pltpu.SMEM)
    vmem = pl.BlockSpec(memory_space=pltpu.VMEM)
    return pl.pallas_call(
        functools.partial(finish_kernel, peers),
        out_shape=(
            jax.ShapeDtypeStruct(wave.shape, jnp.bfloat16),
            jax.ShapeDtypeStruct(wave.shape, jnp.float32),
        ),
        in_specs=[smem, smem, pl.BlockSpec(memory_space=pl.ANY), vmem, vmem],
        out_specs=(vmem, vmem),
        scratch_shapes=[
            pltpu.VMEM(wave.shape, jnp.float32), pltpu.VMEM(wave.shape, jnp.float32),
            pltpu.VMEM(wave.shape, jnp.bfloat16),
            pltpu.VMEM(wave.shape, jnp.float32), pltpu.VMEM(wave.shape, jnp.float32),
            pltpu.VMEM(wave.shape, jnp.bfloat16),
            pltpu.VMEM((16, size), jnp.float32), pltpu.VMEM((peers, 16, size), jnp.float32),
            dma((2,)), dma((sectors,)), dma((sectors,)), dma((sectors,)), dma((sectors,)),
            dma((sectors,)), dma((sectors,)), dma((peers,)), dma((peers,)),
        ],
        compiler_params=pltpu.CompilerParams(collective_id=1, has_side_effects=True,
                                             vmem_limit_bytes=40 * 1024 * 1024),
        name="finish",
    )(rows, cols, sums, wave, energy)


def body(wavefunction, left_env, right_env, energy_diag, sector_dims, pair_table):
    local_sectors = wavefunction.shape[0]
    peer_count = lax.axis_size("sector")
    my_index = lax.axis_index("sector")
    line = my_index // TEAM
    team_sectors = TEAM * local_sectors
    team_first = line * team_sectors
    team_pairs = lax.dynamic_slice_in_dim(pair_table, team_first, team_sectors, 0)
    team_rows = lax.dynamic_slice_in_dim(sector_dims[0], team_first, team_sectors, 0)
    team_cols = jnp.take(sector_dims[1], team_pairs)
    left_all, right_all, wave_all = exchange(wavefunction, left_env, right_env, peer_count)
    sums = products(team_pairs.reshape(-1), team_rows, team_cols.reshape(-1), left_all, right_all, wave_all)
    member_first = (my_index % TEAM) * local_sectors
    rows = lax.dynamic_slice_in_dim(team_rows, member_first, local_sectors, 0)
    cols = lax.dynamic_slice_in_dim(team_cols, member_first, local_sectors, 0)
    return finish(rows, cols.reshape(-1), sums, wavefunction, energy_diag, peer_count)


def solution(mesh):
    blocks = P(("groups", "sector"), None, None, None)
    environments = P(None, ("groups", "sector"), None, None)
    return jax.shard_map(
        body,
        mesh=mesh,
        in_specs=(blocks, environments, environments, blocks, P(), P()),
        out_specs=(blocks, blocks),
        check_vma=False,
    )
```
